32 devices in a mesh: gx: 8 (over z, core), gy: 4 (over y, x).
Axes of the slice: x: 2, y: 2, z: 4, core: 2. Of those that a mesh axis runs over, the one named last changes fastest.
Arguments:
- solution: float32 [512, 4096], P(None, ('gx', 'gy')), may hold values from -6 to 6
- residual: float32 [512, 4096], P(None, ('gx', 'gy')), may hold values from -60 to 60
- metric_diag: bfloat16 [3, 512, 4096], P(None, None, ('gx', 'gy')), may hold values from 0.039794922 to 0.3984375
- metric_cross: bfloat16 [3, 512, 4096], P(None, None, ('gx', 'gy')), may hold values from -0.017944336 to 0.017944336
- fdm_vectors: float32 [3, 8, 8, 4096], P(None, None, None, ('gx', 'gy')), may hold values from -5 to 5
- fdm_values: float32 [3, 8, 4096], P(None, None, ('gx', 'gy')), may hold values from 0.05 to 20
- vertex_ids: int32 [8, 4096], P(None, ('gx', 'gy')), may hold values from 0 to 511
- coarse_inverse: float32 [512, 512], P(('gx', 'gy')), may hold values from -0.2 to 0.2, as said below
- elem_live: int32 [32], P(('gx', 'gy')), may hold values from 80 to 128, as said below
- section_face: int32 [32, 4, 20], P(('gx', 'gy')), may hold values from -1 to 767, as said below
- section_code: int32 [32, 4, 20], P(('gx', 'gy')), may hold values from 0 to 7, as said below
- pipe_face: int32 [32, 2, 64], P(('gx', 'gy')), may hold values from 0 to 767, as said below
- pipe_code: int32 [32, 2, 64], P(('gx', 'gy')), may hold values from 0 to 7, as said below
Outputs:
- solution_out: float32 [512, 4096], P(None, ('gx', 'gy'))
- residual_out: float32 [512, 4096], P(None, ('gx', 'gy'))
- norm_ratio: float32 [1], replicated
The draws below stay inside these ranges and needn't reach their ends.
Inputs may be any that keep to these rules, and one draw needn't show every extreme that they name: `elem_live`: one device holds all 128 slots in every draw. A face id 6 e + f names face f of slot e of the device, with e below the device's elem_live; no id appears twice on a device over section_face and pipe_face; -1 marks an empty slot, and in each peer's row the slots holding faces come first. Slot (q, c) of device (x, y) holds a face exactly when slot (y, c) of device (x, q) does; in the row q = y they come in pairs (c, c xor 1). Each device's rows for peers y - 1, y + 1 and y + 4 / 2 (mod 4) are full; rows for other peers more than two places away (mod 4) are empty. `section_code`: with inv(o) = o for o < 4 and 4 + 2 (o mod 2) + floor((o mod 4) / 2) for o >= 4, the codes of two paired slots are inv of each other; empty slots hold 0. `pipe_face`: every slot holds a face, as for section_face. `pipe_code`: the codes of two paired slots are inv of each other, as for section_code. `coarse_inverse`: Symmetric.
All inputs are finite; a program needn't handle non-finite values.
Results may differ from the reference program's by a relative error of at most 0.0003.
Values sent between devices are 32-bit elements; how exact they have to be, the bound alone decides.
No kernel may reach another device: no remote copies, remote signals or barrier semaphores. Data moves between devices by JAX's collectives and lax.ppermute only.
A program may use at most 64 MiB of HBM per device.

```python
import math
import jax
import jax.numpy as jnp
from jax import lax

EDGE = 8
NPTS = 512
E_DEV = 128
CAP_S = 20
CAP_P = 64
NE = 4096
NV = 512
N_GX = 8
N_GY = 4


def invert_codes(orient_codes):
    return jnp.where(orient_codes >= 4, 4 + 2 * (orient_codes % 2) + orient_codes % 4 // 2, orient_codes)


def face_layout(key):
    base_key = jax.random.fold_in(key, 7)
    device_total = N_GX * N_GY
    key_list = [jax.random.fold_in(base_key, number) for number in range(6)]
    full_device = jax.random.randint(key_list[0], (), 0, device_total)
    alive_count = jax.random.randint(key_list[1], (device_total,), E_DEV * 5 // 8, E_DEV + 1)
    alive_count = jnp.where(jnp.arange(device_total) == full_device, E_DEV, alive_count).astype(jnp.int32)
    drawn_load = jax.random.randint(key_list[2], (N_GX, N_GY, N_GY), CAP_S // 3, CAP_S + 1)
    own_pos = jnp.arange(N_GY)[:, None]
    peer_pos = jnp.arange(N_GY)[None, :]
    slot_load = jnp.where(peer_pos > own_pos, drawn_load, jnp.swapaxes(drawn_load, 1, 2))
    slot_load = jnp.where(peer_pos == own_pos, 2 * (drawn_load // 2), slot_load)
    cycle_gap = jnp.minimum((peer_pos - own_pos) % N_GY, (own_pos - peer_pos) % N_GY)
    beside_pos = (cycle_gap == 1) | (cycle_gap == N_GY // 2)
    slot_load = jnp.where(beside_pos, CAP_S, slot_load)
    slot_load = jnp.where((cycle_gap <= 2) | beside_pos, slot_load, 0).reshape(device_total, N_GY)
    slot_index = jnp.arange(CAP_S)
    live_slot = slot_index[None, None, :] < slot_load[:, :, None]
    offsets = jnp.cumsum(slot_load, axis=1) - slot_load
    section_rank = jnp.minimum(offsets[:, :, None] + slot_index[None, None, :], 6 * E_DEV - 1)
    section_total = jnp.sum(slot_load, axis=1)
    pipe_rank = section_total[:, None, None] + jnp.arange(2)[None, :, None] * CAP_P + jnp.arange(CAP_P)[None, None, :]
    shuffled = jax.vmap(lambda part_key: jax.random.permutation(part_key, 6 * E_DEV))(jax.random.split(key_list[3], device_total))
    face_ids = jnp.arange(6 * E_DEV)
    dead_face = face_ids[None, :] // 6 >= alive_count[:, None]
    scores = shuffled + dead_face.astype(shuffled.dtype) * (6 * E_DEV)
    ordering = jnp.argsort(scores, axis=1, stable=True).astype(jnp.int32)
    picked = jnp.take_along_axis(ordering, section_rank.reshape(device_total, -1), axis=1).reshape(device_total, N_GY, CAP_S)
    section_face = jnp.where(live_slot, picked, -1).astype(jnp.int32)
    pipe_face = jnp.take_along_axis(ordering, pipe_rank.reshape(device_total, -1), axis=1).reshape(device_total, 2, CAP_P).astype(jnp.int32)
    orient_base = jax.random.randint(key_list[4], (N_GX, N_GY, N_GY, CAP_S), 0, 8)
    mirrored = invert_codes(jnp.swapaxes(orient_base, 1, 2))
    section_code = jnp.where((peer_pos > own_pos)[None, :, :, None], orient_base, mirrored)
    even_code = jnp.repeat(orient_base[..., 0::2], 2, axis=-1)
    self_code = jnp.where(slot_index % 2 == 0, even_code, invert_codes(even_code))
    section_code = jnp.where((peer_pos == own_pos)[None, :, :, None], self_code, section_code)
    section_code = jnp.where(live_slot, section_code.reshape(device_total, N_GY, CAP_S), 0).astype(jnp.int32)
    upward = jax.random.randint(key_list[5], (N_GX, N_GY, CAP_P), 0, 8)
    downward = invert_codes(jnp.roll(upward, 1, axis=0))
    pipe_code = jnp.stack([downward, upward], axis=2).reshape(device_total, 2, CAP_P).astype(jnp.int32)
    return (alive_count, section_face, section_code, pipe_face, pipe_code)


def draw_elem_live(key, part):
    return face_layout(key)[0]


def draw_section_face(key, part):
    return face_layout(key)[1]


def draw_section_code(key, part):
    return face_layout(key)[2]


def draw_pipe_face(key, part):
    return face_layout(key)[3]


def draw_pipe_code(key, part):
    return face_layout(key)[4]


def draw_residual(key, part):
    values = jnp.clip(jax.random.normal(jax.random.fold_in(key, 3), (NPTS, NE), jnp.float32), -4.0, 4.0)
    device = (jnp.arange(NE) // E_DEV).astype(jnp.float32)
    rising = 1.0 + 2.0 * device / max(N_GX * N_GY - 1, 1)
    return values * rising[None, :]


def draw_coarse_inverse(key, part):
    raw_values = jnp.clip(jax.random.normal(jax.random.fold_in(key, 9), (NV, NV), jnp.float32), -4.0, 4.0)
    symmetric = (raw_values + raw_values.T) * (0.7 * 0.07 / math.sqrt(NV))
    diagonal = 0.07 + 0.07 * jax.random.uniform(jax.random.fold_in(key, 10), (NV,), jnp.float32)
    return symmetric + jnp.eye(NV, dtype=jnp.float32) * diagonal[None, :]


def place_ends(drawn, own_key, smallest, high):
    shape = drawn.shape
    spot = [jax.random.randint(jax.random.fold_in(own_key, axis), (), 0, shape[axis]) for axis in range(len(shape))]
    drawn = drawn.at[tuple(spot)].set(smallest)
    longest = shape.index(max(shape))
    spot[longest] = (spot[longest] + 1) % shape[longest]
    return drawn.at[tuple(spot)].set(high)


def shard_levels(own_key, shape, cuts, smallest, top_value):
    def one(axis_at, parts):
        heights = jax.random.uniform(jax.random.fold_in(jax.random.fold_in(own_key, 6), axis_at), (parts,), jnp.float32, smallest / len(cuts), top_value / len(cuts))
        return jnp.repeat(jnp.exp(heights), shape[axis_at] // parts).reshape((-1,) + (1,) * (len(shape) - axis_at - 1))

    loudness = one(*cuts[0])
    for cut in cuts[1:]:
        loudness = loudness * one(*cut)
    return loudness


def normal_values(key, dims, deviation, bound, cuts=(), held_as=jnp.bfloat16):
    result = deviation * jax.random.normal(key, dims, jnp.float32)
    if cuts:
        result = result * shard_levels(key, dims, cuts, -0.22, 0.18)
    return jnp.clip(result, -bound, bound).astype(held_as)


def setup_inputs(seed: int = 0) -> dict:
    key_of = jax.random.split(jax.random.key(seed), 14)
    solution = normal_values(key_of[0], (NPTS, NE), 1.0, 6.0, ((1, 32),), jnp.float32)
    residual = draw_residual(jax.random.fold_in(key_of[13], 71), 0)
    metric_diag = jnp.clip(jnp.exp(math.log(0.3984375) - 2.3038113 * jax.random.uniform(key_of[2], (3, NPTS, NE), jnp.float32) ** shard_levels(key_of[2], (3, NPTS, NE), ((2, 32),), -0.2, 0.2)), 0.039794922, 0.3984375).astype(jnp.bfloat16)
    metric_cross = jnp.clip(jax.random.uniform(key_of[3], (3, NPTS, NE), jnp.float32, -0.017944336, 0.017944336) * shard_levels(key_of[3], (3, NPTS, NE), ((2, 32),), -0.4, 0.0), -0.017944336, 0.017944336).astype(jnp.bfloat16)
    fdm_vectors = normal_values(key_of[4], (3, EDGE, EDGE, NE), 0.35, 5.0, ((3, 32),), jnp.float32)
    fdm_values = jnp.clip(jnp.exp(math.log(20.0) - 5.9914645 * jax.random.uniform(key_of[5], (3, EDGE, NE), jnp.float32) ** shard_levels(key_of[5], (3, EDGE, NE), ((2, 32),), -0.2, 0.2)), 0.05, 20.0)
    vertex_ids = place_ends(jax.random.randint(key_of[6], (8, NE), 0, NV), jax.random.fold_in(key_of[6], 1), 0, NV - 1).astype(jnp.int32)
    coarse_inverse = draw_coarse_inverse(jax.random.fold_in(key_of[13], 71), 0)
    elem_live = draw_elem_live(jax.random.fold_in(key_of[13], 71), 0)
    section_face = draw_section_face(jax.random.fold_in(key_of[13], 71), 0)
    section_code = draw_section_code(jax.random.fold_in(key_of[13], 71), 0)
    pipe_face = draw_pipe_face(jax.random.fold_in(key_of[13], 71), 0)
    pipe_code = draw_pipe_code(jax.random.fold_in(key_of[13], 71), 0)
    return dict(solution=solution, residual=residual, metric_diag=metric_diag, metric_cross=metric_cross, fdm_vectors=fdm_vectors, fdm_values=fdm_values, vertex_ids=vertex_ids, coarse_inverse=coarse_inverse, elem_live=elem_live, section_face=section_face, section_code=section_code, pipe_face=pipe_face, pipe_code=pipe_code)


top_precision = lax.Precision.HIGHEST


def node_points():
    node_index = jnp.arange(EDGE).astype(jnp.float32)
    return -jnp.cos(jnp.pi * node_index / (EDGE - 1))


def derivative_matrix():
    points = node_points()
    node_index = jnp.arange(EDGE)
    weights = jnp.where((node_index == 0) | (node_index == EDGE - 1), 2.0, 1.0).astype(jnp.float32)
    parity = jnp.where((node_index[:, None] + node_index[None, :]) % 2 == 0, 1.0, -1.0).astype(jnp.float32)
    identity = jnp.eye(EDGE, dtype=jnp.float32)
    spacing = points[:, None] - points[None, :] + identity
    offdiag = (weights[:, None] / weights[None, :]) * parity / spacing * (1.0 - identity)
    return offdiag - jnp.diag(jnp.sum(offdiag, axis=1))


def corner_table():
    points = node_points()
    hat_values = jnp.stack([(1.0 - points) * 0.5, (1.0 + points) * 0.5])
    corner_weights = hat_values[:, None, None, :, None, None] * hat_values[None, :, None, None, :, None] * hat_values[None, None, :, None, None, :]
    return corner_weights.reshape(8, EDGE ** 3)


def orient_faces(face_rows, orient_codes):
    face_grid = face_rows.reshape(-1, EDGE, EDGE)
    face_grid = jnp.where((orient_codes % 2 == 1)[:, None, None], face_grid[:, ::-1, :], face_grid)
    face_grid = jnp.where(((orient_codes // 2) % 2 == 1)[:, None, None], face_grid[:, :, ::-1], face_grid)
    face_grid = jnp.where((orient_codes >= 4)[:, None, None], jnp.swapaxes(face_grid, 1, 2), face_grid)
    return face_grid.reshape(-1, EDGE * EDGE)


def face_slabs(element_cube):
    stacked = jnp.stack([element_cube[0], element_cube[EDGE - 1], element_cube[:, 0], element_cube[:, EDGE - 1], element_cube[:, :, 0], element_cube[:, :, EDGE - 1]])
    return jnp.transpose(stacked, (3, 0, 1, 2)).reshape(-1, EDGE * EDGE)


def add_slabs(element_cube, face_extra):
    face_parts = jnp.transpose(face_extra.reshape(-1, 6, EDGE, EDGE), (1, 2, 3, 0))
    element_cube = element_cube.at[0].add(face_parts[0])
    element_cube = element_cube.at[EDGE - 1].add(face_parts[1])
    element_cube = element_cube.at[:, 0].add(face_parts[2])
    element_cube = element_cube.at[:, EDGE - 1].add(face_parts[3])
    element_cube = element_cube.at[:, :, 0].add(face_parts[4])
    element_cube = element_cube.at[:, :, EDGE - 1].add(face_parts[5])
    return element_cube


def scatter_faces(face_count, targets, face_rows):
    placed = jnp.where(targets < 0, face_count, targets).astype(jnp.int32)
    return jnp.zeros((face_count, EDGE * EDGE), dtype=face_rows.dtype).at[placed].add(face_rows, mode="drop")


def fdm_solve(element_cube, vectors, values):
    spectral = jnp.einsum("iae,ijke->ajke", vectors[0], element_cube, precision=top_precision)
    spectral = jnp.einsum("jbe,ajke->abke", vectors[1], spectral, precision=top_precision)
    spectral = jnp.einsum("kce,abke->abce", vectors[2], spectral, precision=top_precision)
    eigen_sums = values[0][:, None, None, :] + values[1][None, :, None, :] + values[2][None, None, :, :]
    spectral = spectral / eigen_sums
    restored = jnp.einsum("iae,abce->ibce", vectors[0], spectral, precision=top_precision)
    restored = jnp.einsum("jbe,ibce->ijce", vectors[1], restored, precision=top_precision)
    return jnp.einsum("kce,ijce->ijke", vectors[2], restored, precision=top_precision)


def local_operator(field, diag_part, cross_part, derivative):
    element_cube = field.reshape(EDGE, EDGE, EDGE, -1)
    diagonal = diag_part.astype(jnp.float32).reshape(3, EDGE, EDGE, EDGE, -1)
    cross_terms = cross_part.astype(jnp.float32).reshape(3, EDGE, EDGE, EDGE, -1)
    grad_first = jnp.einsum("ai,ijke->ajke", derivative, element_cube, precision=top_precision)
    grad_second = jnp.einsum("aj,ijke->iake", derivative, element_cube, precision=top_precision)
    grad_third = jnp.einsum("ak,ijke->ijae", derivative, element_cube, precision=top_precision)
    flux_first = diagonal[0] * grad_first + cross_terms[0] * grad_second + cross_terms[1] * grad_third
    flux_second = cross_terms[0] * grad_first + diagonal[1] * grad_second + cross_terms[2] * grad_third
    flux_third = cross_terms[1] * grad_first + cross_terms[2] * grad_second + diagonal[2] * grad_third
    curvature = jnp.sum(grad_first * flux_first + grad_second * flux_second + grad_third * flux_third) + jnp.sum(element_cube * element_cube)
    applied = jnp.einsum("ai,ajke->ijke", derivative, flux_first, precision=top_precision)
    applied = applied + jnp.einsum("aj,iake->ijke", derivative, flux_second, precision=top_precision)
    applied = applied + jnp.einsum("ak,ijae->ijke", derivative, flux_third, precision=top_precision)
    return (applied + element_cube).reshape(EDGE ** 3, -1), curvature


def by_device(function, arrays):
    folded = tuple(jnp.moveaxis(member.reshape(member.shape[:-1] + (N_GX * N_GY, E_DEV)), -2, 0) for member in arrays)
    return lax.map(lambda grouped: function(*grouped), folded)


def unfold(member):
    return jnp.moveaxis(member, 0, -2).reshape(member.shape[1:-1] + (-1,))


def face_sum(field, section_face, section_code, pipe_face, pipe_code):
    element_cube = field.reshape(EDGE, EDGE, EDGE, -1)
    face_values = face_slabs(element_cube)
    per_device = 6 * E_DEV
    device = jnp.arange(N_GX * N_GY).astype(jnp.int32)
    row_pos = device // N_GY
    col_pos = device % N_GY
    peer_index = jnp.arange(N_GY).astype(jnp.int32)
    slot_index = jnp.arange(CAP_S).astype(jnp.int32)
    partner_dev = row_pos[:, None, None] * N_GY + peer_index[None, :, None]
    same_peer = peer_index[None, :, None] == col_pos[:, None, None]
    partner_slot = jnp.where(same_peer, slot_index[None, None, :] + 1 - 2 * (slot_index[None, None, :] % 2), slot_index[None, None, :])
    partner_face = section_face[partner_dev, col_pos[:, None, None], partner_slot]
    source = (partner_dev * per_device + jnp.maximum(partner_face, 0)).astype(jnp.int32)
    incoming = orient_faces(face_values[source.reshape(-1)], section_code.reshape(-1))
    target = jnp.where(section_face >= 0, device[:, None, None] * per_device + section_face, -1).reshape(-1).astype(jnp.int32)
    side_index = jnp.arange(2).astype(jnp.int32)
    pipe_row = (row_pos[:, None] - 1 + 2 * side_index[None, :]) % N_GX
    pipe_dev = pipe_row * N_GY + col_pos[:, None]
    pipe_partner = pipe_face[pipe_dev[:, :, None], (1 - side_index)[None, :, None], jnp.arange(CAP_P).astype(jnp.int32)[None, None, :]]
    pipe_source = (pipe_dev[:, :, None] * per_device + pipe_partner).astype(jnp.int32)
    beside = orient_faces(face_values[pipe_source.reshape(-1)], pipe_code.reshape(-1))
    pipe_target = (device[:, None, None] * per_device + pipe_face).reshape(-1).astype(jnp.int32)
    face_extra = scatter_faces(face_values.shape[0], jnp.concatenate([target, pipe_target]), jnp.concatenate([incoming, beside]))
    return add_slabs(element_cube, face_extra).reshape(EDGE ** 3, -1)


def reference(solution, residual, metric_diag, metric_cross, fdm_vectors, fdm_values, vertex_ids, coarse_inverse, elem_live, section_face, section_code, pipe_face, pipe_code):
    slot_index = jnp.arange(N_GX * N_GY * E_DEV).astype(jnp.int32)
    alive_mask = (slot_index % E_DEV < elem_live[slot_index // E_DEV]).astype(jnp.float32)
    rmask = residual * alive_mask[None, :]
    corner_weights = corner_table()
    derivative = derivative_matrix()
    corners = jnp.dot(corner_weights, rmask, precision=top_precision)
    coarse_rhs = jax.ops.segment_sum(corners.reshape(-1), vertex_ids.reshape(-1), num_segments=NV)
    coarse_sol = jnp.dot(coarse_inverse, coarse_rhs, precision=top_precision)
    smooth = unfold(by_device(lambda vectors_part, values_part, field_part: fdm_solve(field_part.reshape(EDGE, EDGE, EDGE, -1), vectors_part, values_part).reshape(EDGE ** 3, -1), (fdm_vectors, fdm_values, rmask)))
    summed = face_sum(smooth, section_face, section_code, pipe_face, pipe_code)
    lifted = jnp.dot(corner_weights.T, coarse_sol[vertex_ids], precision=top_precision)
    direction = alive_mask[None, :] * (summed + lifted)
    applied_parts, curvature_parts = by_device(lambda field_part, diag_part, cross_part: local_operator(field_part, diag_part, cross_part, derivative), (direction, metric_diag, metric_cross))
    curvature = jnp.sum(curvature_parts)
    image = face_sum(unfold(applied_parts), section_face, section_code, pipe_face, pipe_code)
    precond_dot = jnp.sum(rmask * direction)
    old_norm = jnp.sum(rmask * rmask)
    step_length = precond_dot / curvature
    solution_out = alive_mask[None, :] * (solution + step_length * direction)
    residual_out = rmask - step_length * image
    norm_ratio = jnp.sum(residual_out * residual_out) / old_norm
    return solution_out, residual_out, norm_ratio.reshape(1)
```

```python
import functools

import jax
import jax.numpy as jnp
import numpy as np
from jax import lax
from jax.experimental import pallas as pl
from jax.experimental.pallas import tpu as pltpu
from jax.sharding import PartitionSpec as P

EDGE = 8
PLANE = EDGE * EDGE
POINTS = EDGE**3
FACES = 6
CORNERS = 8
LANES = 128
AXES = ("gx", "gy")
DIRECT_BYTES = 1 << 20

exact = lax.Precision.HIGHEST
f32 = jnp.float32
bf16 = jnp.bfloat16


def node_tables():
    index = np.arange(EDGE)
    points = -np.cos(np.pi * index / (EDGE - 1))
    ends = np.where((index == 0) | (index == EDGE - 1), 2.0, 1.0)
    derivative = np.zeros((EDGE, EDGE))
    for a in range(EDGE):
        for b in range(EDGE):
            if a != b:
                derivative[a, b] = ends[a] / ends[b] * (-1.0) ** (a + b) / (points[a] - points[b])
    derivative -= np.diag(derivative.sum(axis=1))
    hats = np.stack([(1.0 - points) / 2, (1.0 + points) / 2])
    return derivative, hats


DERIVATIVE, HATS = node_tables()


TALL = POINTS + EDGE


def number(value):
    return float(np.float32(value))


def pairings(count):
    ring = np.arange(count)
    return [ring ^ 1, (((ring + 1) ^ 1) - 1) % count]


def section_pairings(count):
    ring = np.arange(count)
    found = []
    for table in [
        *pairings(count),
        (ring + count // 2) % count,
        ring ^ 2,
        (((ring + 2) ^ 2) - 2) % count,
    ]:
        if not any(np.array_equal(table, other) for other in found):
            found.append(table)
    return found


def chosen(table, own):
    value = jnp.int32(table[0])
    for place in range(1, len(table)):
        value = jnp.where(own == place, jnp.int32(table[place]), value)
    return value


def lane_index(rows=1, width=LANES):
    return lax.broadcasted_iota(jnp.int32, (rows, width), 1)


def halves(values):
    top = values.astype(bf16)
    rest = (values - top.astype(f32)).astype(bf16)
    return jnp.concatenate([top, rest], axis=0)


def joined(product):
    rows = product.shape[0] // 2
    return product[:rows] + product[rows:]


def pad_lanes(row, width, fill):
    if row.shape[1] == width:
        return row
    return jnp.concatenate([row, jnp.full((1, width - row.shape[1]), fill, row.dtype)], axis=1)


def added(members):
    members = list(members)
    while len(members) > 1:
        pairs = [left + right for left, right in zip(members[0::2], members[1::2])]
        members = pairs + members[2 * len(pairs) :]
    return members[0]


def fold(values):
    return added(
        [values[row : row + EDGE] for row in range(0, values.shape[0], EDGE)]
    )


def total_of(values):
    return jnp.sum(jnp.sum(fold(values), axis=0, keepdims=True), axis=1, keepdims=True)


def lane_row(members):
    lanes = lane_index()
    row = jnp.zeros((1, LANES), f32)
    for place, member in enumerate(members):
        row = jnp.where(lanes == place, member, row)
    return row


def begin(copies):
    started = [pltpu.make_async_copy(*copy) for copy in copies]
    for copy in started:
        copy.start()
    return started


def section_row(table_ref, fill):
    peers, capacity = table_ref.shape
    own = lax.axis_index("gy")
    partners = [own] + [chosen(table, own) for table in section_pairings(peers)]
    rows = [table_ref[pl.ds(partner, 1), :] for partner in partners]
    width = -(-len(rows) * capacity // LANES) * LANES
    return pad_lanes(jnp.concatenate(rows, axis=1), width, fill)


def pipe_row(table_ref):
    side = lax.rem(lax.axis_index("gx"), 2)
    return jnp.concatenate(
        [table_ref[pl.ds(1 - side, 1), :], table_ref[pl.ds(side, 1), :]], axis=1
    )


def face_columns(ids, slots):
    element = ids // FACES
    return jnp.where(ids < 0, -1, (ids - element * FACES) * slots + element)


def slot_columns(slots, section_ref, pipe_ref):
    ids = jnp.concatenate([section_row(section_ref, -1), pipe_row(pipe_ref)], axis=1)
    return face_columns(ids, slots)


def slot_codes(section_code_ref, pipe_code_ref):
    codes = jnp.concatenate([section_row(section_code_ref, 0), pipe_row(pipe_code_ref)], axis=1)
    return jnp.broadcast_to(codes, (EDGE, codes.shape[1]))


def one_hot(columns, height):
    rows = lax.broadcasted_iota(jnp.int32, (height, columns.shape[1]), 0)
    return jnp.where(rows == columns, 1.0, 0.0).astype(bf16)


def pick_faces(cube_ref, hot_ref, capacity, section_out, pipe_out):
    last = EDGE - 1
    faces = [
        cube_ref[0:PLANE, :],
        cube_ref[last * PLANE : EDGE * PLANE, :],
        jnp.concatenate([cube_ref[i * PLANE : i * PLANE + EDGE, :] for i in range(EDGE)], axis=0),
        jnp.concatenate(
            [cube_ref[(i + 1) * PLANE - EDGE : (i + 1) * PLANE, :] for i in range(EDGE)], axis=0
        ),
        cube_ref[pl.ds(0, PLANE, stride=EDGE), :],
        cube_ref[pl.ds(last, PLANE, stride=EDGE), :],
    ]
    values = halves(jnp.concatenate(faces, axis=1))
    picked = joined(jnp.dot(values, hot_ref[...], preferred_element_type=f32))
    width = section_out.shape[1]
    pipe_out[...] = picked[:, width:]
    section = picked[:, :width]
    first = section[:, :LANES]
    after = pltpu.roll(first, LANES - 1, axis=1)
    before = pltpu.roll(first, 1, axis=1)
    lanes = lane_index()
    paired = jnp.where(lanes % 2 == 0, after, before)
    section_out[...] = section
    section_out[:, :LANES] = jnp.where(lanes < capacity, paired, first)


def section_columns(capacity, block_refs, order):
    own_ref, *arrived = block_refs
    lanes = lane_index(1, own_ref.shape[1])
    section = own_ref[...]
    for place, member_ref in zip(order, arrived):
        start = (place + 1) * capacity
        section = jnp.where(
            (lanes >= start) & (lanes < start + capacity), member_ref[...], section
        )
    return section


def pipe_columns(first_ref, second_ref):
    half = first_ref.shape[1] // 2
    return jnp.where(lane_index(1, 2 * half) < half, first_ref[...], second_ref[...])


def packed_height(capacity):
    return -(-EDGE // (LANES // capacity)) * EDGE


def pack_section(section, place, capacity):
    beside = LANES // capacity
    lanes = lane_index()
    tiles = [jnp.zeros((EDGE, LANES), f32)] * (packed_height(capacity) // EDGE)
    for a in range(EDGE):
        start = a % beside * capacity
        moved = pltpu.roll(
            section[a * EDGE : (a + 1) * EDGE], (start - place * capacity) % LANES, axis=1
        )
        inside = (lanes >= start) & (lanes < start + capacity)
        tiles[a // beside] = jnp.where(inside, moved, tiles[a // beside])
    return stacked(tiles)


def unpacked_section(own, blocks, order, capacity):
    beside = LANES // capacity
    lanes = lane_index()
    rows = [own[a * EDGE : (a + 1) * EDGE] for a in range(EDGE)]
    for place, block in zip(order, blocks):
        start = (place + 1) * capacity
        inside = (lanes >= start) & (lanes < start + capacity)
        for a in range(EDGE):
            tile = block[a // beside * EDGE : (a // beside + 1) * EDGE]
            moved = pltpu.roll(tile, (start - a % beside * capacity) % LANES, axis=1)
            rows[a] = jnp.where(inside, moved, rows[a])
    return stacked(rows)


def pack_pipes(pipe):
    half = PLANE // 2
    first = lane_index() < LANES // 2
    top, bottom = pipe[:half], pipe[half:]
    near = jnp.where(first, top, pltpu.roll(bottom, LANES // 2, axis=1))
    far = jnp.where(first, pltpu.roll(top, LANES // 2, axis=1), bottom)
    return near, far


def unpacked_pipes(near, far):
    first = lane_index() < LANES // 2
    top = jnp.where(first, near, pltpu.roll(far, LANES // 2, axis=1))
    bottom = jnp.where(first, pltpu.roll(near, LANES // 2, axis=1), far)
    return stacked([top, bottom])


def add_faces(cube_ref, grid_ref, codes_ref, hot_ref, values, start):
    slots = cube_ref.shape[1]
    last = EDGE - 1
    columns_used = slice(start, start + values.shape[1])
    codes = codes_ref[:, columns_used]
    odd = codes & 1 == 1
    second = codes & 2 == 2
    turned = codes >= 4
    turned_groups = []
    for group in range(values.shape[1] // LANES):
        span = slice(group * LANES, (group + 1) * LANES)
        base = group * PLANE
        whole = slice(base, base + PLANE)
        across = [pl.ds(base + b, EDGE, stride=EDGE) for b in range(EDGE)]
        rows = [values[a * EDGE : (a + 1) * EDGE, span] for a in range(EDGE)]
        rows = [jnp.where(odd[:, span], rows[last - a], rows[a]) for a in range(EDGE)]
        grid_ref[whole, :] = stacked(rows)
        columns = [grid_ref[place, :] for place in across]
        columns = [
            jnp.where(second[:, span], columns[last - b], columns[b]) for b in range(EDGE)
        ]
        grid_ref[whole, :] = stacked(columns)
        rows = [grid_ref[place, :] for place in across]
        rows = [jnp.where(turned[:, span], columns[a], rows[a]) for a in range(EDGE)]
        turned_groups.append(stacked(rows))
    grid = halves(jnp.concatenate(turned_groups, axis=1))
    extra = joined(
        lax.dot_general(
            grid, hot_ref[:, columns_used], (((1,), (1,)), ((), ())), preferred_element_type=f32
        )
    )
    parts = [extra[:, face * slots : (face + 1) * slots] for face in range(FACES)]
    cube_ref[0:PLANE, :] += parts[0]
    cube_ref[last * PLANE : EDGE * PLANE, :] += parts[1]
    for i in range(EDGE):
        piece = slice(i * EDGE, (i + 1) * EDGE)
        cube_ref[i * PLANE : i * PLANE + EDGE, :] += parts[2][piece]
        cube_ref[(i + 1) * PLANE - EDGE : (i + 1) * PLANE, :] += parts[3][piece]
    cube_ref[pl.ds(0, PLANE, stride=EDGE), :] += parts[4]
    cube_ref[pl.ds(last, PLANE, stride=EDGE), :] += parts[5]


def hat_pattern(side, slots):
    index = lax.broadcasted_iota(jnp.int32, (EDGE, slots), 0)
    pattern = jnp.full((EDGE, slots), number(HATS[side, 0]), f32)
    for k in range(1, EDGE):
        pattern = jnp.where(index == k, number(HATS[side, k]), pattern)
    return pattern


def hat_sum(side, members):
    total = None
    for weight, member in zip(HATS[side], members):
        if weight:
            term = member if weight == 1.0 else number(weight) * member
            total = term if total is None else total + term
    return total


def corner_sums(cube_ref):
    slots = cube_ref.shape[1]
    patterns = [hat_pattern(side, slots) for side in range(2)]
    rows = []
    for first in range(2):
        plane = hat_sum(first, [cube_ref[i * PLANE : (i + 1) * PLANE, :] for i in range(EDGE)])
        for second in range(2):
            line = hat_sum(second, [plane[j * EDGE : (j + 1) * EDGE] for j in range(EDGE)])
            for third in range(2):
                rows.append(jnp.sum(line * patterns[third], axis=0, keepdims=True))
    return rows


def hat_pair(pair, index):
    low, high = HATS[:, index]
    if high == 0.0:
        return pair[0]
    if low == 0.0:
        return pair[1]
    return number(low) * pair[0] + number(high) * pair[1]


def stacked(members):
    return jnp.concatenate(members, axis=0)


def lift_corners(rows, slots):
    patterns = [hat_pattern(side, slots) for side in range(2)]
    planes, slopes, rises = [], [], []
    for first in range(2):
        corners = [rows[4 * first + c] for c in range(4)]
        lines = [corners[2 * j] * patterns[0] + corners[2 * j + 1] * patterns[1] for j in range(2)]
        planes.append(stacked([hat_pair(lines, j) for j in range(EDGE)]))
        slopes.append(0.5 * (lines[1] - lines[0]))
        steps = [0.5 * (corners[2 * j + 1] - corners[2 * j]) for j in range(2)]
        rises.append(stacked([hat_pair(steps, j) for j in range(EDGE)]))
    field = [hat_pair(planes, i) for i in range(EDGE)]
    along_first = 0.5 * (planes[1] - planes[0])
    along_second = stacked([hat_pair(slopes, i) for i in range(EDGE)])
    along_third = stacked([hat_pair(rises, i) for i in range(EDGE)])
    return field, along_first, along_second, along_third


def coarse_terms(rows, vertex_ref, pieces):
    ids = corner_ids(vertex_ref)
    weights = jnp.concatenate(rows, axis=1)
    tall = max(pieces, EDGE)
    high = lax.broadcasted_iota(jnp.int32, (tall, ids.shape[1]), 0) == ids // LANES
    low = lax.broadcasted_iota(jnp.int32, (LANES, ids.shape[1]), 0) == ids % LANES
    total = joined(
        lax.dot_general(
            halves(jnp.where(high, weights, 0.0)),
            jnp.where(low, 1.0, 0.0).astype(bf16),
            (((1,), (1,)), ((), ())),
            preferred_element_type=f32,
        )
    )
    return total[:pieces]


def corner_ids(vertex_ref):
    return jnp.concatenate([vertex_ref[c : c + 1, :] for c in range(CORNERS)], axis=1)


def coarse_lookup(table, low_ref, high_ref, slots):
    taken = joined(jnp.dot(halves(table), low_ref[...], preferred_element_type=f32))
    taken = jnp.sum(taken * high_ref[...], axis=0, keepdims=True)
    return [taken[:, c * slots : (c + 1) * slots] for c in range(CORNERS)]


def smooth_kernel(
    live_ref,
    section_hbm,
    pipe_hbm,
    vectors_hbm,
    residual_hbm,
    values_hbm,
    vertex_hbm,
    terms_hbm,
    rmask_ref,
    smooth_ref,
    section_out,
    pipe_out,
    alive_ref,
    hot_ref,
    vertex_ref,
    corners_ref,
    section_ref,
    pipe_ref,
    vectors_ref,
    values_ref,
    spread_ref,
    first_ref,
    second_ref,
    terms_ref,
    arrivals,
):
    slots = rmask_ref.shape[1]
    targets = [
        (section_hbm, section_ref),
        (pipe_hbm, pipe_ref),
        (vectors_hbm, vectors_ref),
        (residual_hbm, rmask_ref),
        (values_hbm, values_ref),
        (vertex_hbm, vertex_ref),
    ]
    copies = begin(
        [(source, target, arrivals.at[n]) for n, (source, target) in enumerate(targets)]
    )
    alive = jnp.where(lane_index(1, slots) < live_ref[0], 1.0, 0.0)
    alive_ref[...] = alive
    for copy in copies[:2]:
        copy.wait()
    hot_ref[...] = one_hot(slot_columns(slots, section_ref, pipe_ref), FACES * slots)
    copies[2].wait()

    def spread(step, carry):
        block = vectors_ref[pl.ds(pl.multiple_of(step * EDGE, EDGE), EDGE), :]
        for row in range(EDGE):
            spread_ref[step * EDGE + row] = jnp.broadcast_to(block[row : row + 1], (EDGE, slots))
        return carry

    lax.fori_loop(0, 3 * EDGE, spread, 0)
    for copy in copies[3:]:
        copy.wait()
    rmask_ref[...] = rmask_ref[...] * alive
    rows = corner_sums(rmask_ref)
    corners_ref[...] = stacked(rows)
    terms = coarse_terms(rows, vertex_ref, terms_ref.shape[1])
    terms_ref[...] = jnp.broadcast_to(terms[None], terms_ref.shape)
    (departure,) = begin([(terms_ref, terms_hbm, arrivals.at[len(copies)])])

    def mix(direction, lines, turned):
        results = [[] for _ in lines]
        for a in range(EDGE):
            totals = [None] * len(lines)
            for b in range(EDGE):
                pair = a * EDGE + b if turned else b * EDGE + a
                weight = spread_ref[direction * PLANE + pair]
                for place, line in enumerate(lines):
                    term = weight * line[b]
                    totals[place] = term if b == 0 else totals[place] + term
            for result, total in zip(results, totals):
                result.append(total)
        return results

    def load(ref, places):
        return [[ref[place, :] for place in line] for line in places]

    def store(ref, places, lines):
        for line, members in zip(places, lines):
            for place, member in zip(line, members):
                ref[place, :] = member

    pair_of = range(2)

    def along_first(source_ref, target_ref, turned):
        def body(step, carry):
            at = [
                [
                    pl.ds(pl.multiple_of(i * PLANE + (2 * step + n) * EDGE, EDGE), EDGE)
                    for i in range(EDGE)
                ]
                for n in pair_of
            ]
            store(target_ref, at, mix(0, load(source_ref, at), turned))
            return carry

        lax.fori_loop(0, EDGE // 2, body, 0)

    along_first(rmask_ref, first_ref, False)

    def body(step, carry):
        bases = [pl.multiple_of((2 * step + n) * PLANE, PLANE) for n in pair_of]
        at = [[pl.ds(base + j * EDGE, EDGE) for j in range(EDGE)] for base in bases]
        across = [[pl.ds(base + k, EDGE, stride=EDGE) for k in range(EDGE)] for base in bases]
        store(second_ref, at, mix(1, load(first_ref, at), False))
        lines = mix(2, load(second_ref, across), False)
        for n in pair_of:
            shared = values_ref[pl.ds(2 * step + n, 1), :] + values_ref[EDGE : 2 * EDGE, :]
            lines[n] = [
                member / (shared + values_ref[2 * EDGE + c : 2 * EDGE + c + 1, :])
                for c, member in enumerate(lines[n])
            ]
        store(first_ref, across, mix(2, lines, True))
        store(second_ref, at, mix(1, load(first_ref, at), True))
        return carry

    lax.fori_loop(0, EDGE // 2, body, 0)
    along_first(second_ref, smooth_ref, True)
    pick_faces(smooth_ref, hot_ref, section_ref.shape[1], section_out, pipe_out)
    departure.wait()


def coarse_rows_kernel(inverse_ref, parts_ref, out_ref):
    total = added([parts_ref[device] for device in range(parts_ref.shape[0])])
    rows, vertices = inverse_ref.shape
    products = added(
        [
            inverse_ref[:, piece * LANES : (piece + 1) * LANES] * total[piece : piece + 1]
            for piece in range(vertices // LANES)
        ]
    )
    sums = jnp.broadcast_to(jnp.sum(products, axis=1, keepdims=True), (rows, LANES))
    own = lax.broadcasted_iota(jnp.int32, (rows, LANES), 0) == lane_index(rows)
    row = jnp.sum(jnp.where(own, sums, 0.0), axis=0, keepdims=True)
    out_ref[...] = jnp.broadcast_to(row, out_ref.shape)


def combine(matrix, values):
    half = EDGE // 2
    last = EDGE - 1
    sums = [values[b] + values[last - b] for b in range(half)]
    gaps = [values[b] - values[last - b] for b in range(half)]
    results = [None] * EDGE
    for a in range(half):
        even = sum(
            number(0.5 * (matrix[a, b] + matrix[a, last - b])) * sums[b] for b in range(half)
        )
        odd = sum(
            number(0.5 * (matrix[a, b] - matrix[a, last - b])) * gaps[b] for b in range(half)
        )
        results[a] = odd + even
        results[last - a] = odd - even
    return results


def face_kernel(
    blocks,
    capacity,
    own_rows,
    diagonal_hbm,
    cross_hbm,
    section_code_hbm,
    pipe_code_hbm,
    smooth_ref,
    rmask_ref,
    vertex_ref,
    alive_ref,
    hot_ref,
    *refs,
):
    block_refs, refs = refs[:blocks], refs[blocks:]
    part_ref, first_ref, second_ref, third_ref, diagonal_ref, cross_ref, *refs = refs
    sums_ref, low_ref, high_ref, codes_ref, grid_ref, *refs = refs
    section_code_ref, pipe_code_ref, arrivals = refs
    copies = begin(
        [
            (section_code_hbm, section_code_ref, arrivals.at[0]),
            (pipe_code_hbm, pipe_code_ref, arrivals.at[1]),
            (diagonal_hbm, diagonal_ref, arrivals.at[2]),
            (cross_hbm, cross_ref, arrivals.at[3]),
        ]
    )
    rmask = rmask_ref[...]
    sums_ref[EDGE : 2 * EDGE, :] = fold(rmask * rmask)
    ids = corner_ids(vertex_ref)
    low = lax.broadcasted_iota(jnp.int32, low_ref.shape, 0) == ids % own_rows
    high = lax.broadcasted_iota(jnp.int32, high_ref.shape, 0) == ids // own_rows
    low_ref[...] = jnp.where(low, 1.0, 0.0).astype(bf16)
    high_ref[...] = jnp.where(high, 1.0, 0.0)
    part_ref[:POINTS, :] = smooth_ref[:POINTS, :]
    for copy in copies[:2]:
        copy.wait()
    codes_ref[...] = slot_codes(section_code_ref, pipe_code_ref)
    own_ref, far_ref, near_ref, *arrived = block_refs
    order = arrival_order(len(arrived))
    section = section_columns(capacity, [own_ref, *arrived], order)
    values = jnp.concatenate([section, pipe_columns(near_ref, far_ref)], axis=1)
    add_faces(part_ref, grid_ref, codes_ref, hot_ref, values, 0)
    alive = alive_ref[...]
    part_ref[:POINTS, :] = alive * part_ref[:POINTS, :]

    def gradient(step, carry):
        base = pl.multiple_of(step * PLANE, PLANE)
        row = pl.multiple_of(step * EDGE, EDGE)
        for target_ref, places in (
            (first_ref, [pl.ds(i * PLANE + row, EDGE) for i in range(EDGE)]),
            (second_ref, [pl.ds(base + j * EDGE, EDGE) for j in range(EDGE)]),
            (third_ref, [pl.ds(base + k, EDGE, stride=EDGE) for k in range(EDGE)]),
        ):
            values = combine(DERIVATIVE, [part_ref[place, :] for place in places])
            for place, member in zip(places, values):
                target_ref[place, :] = member
        return carry

    lax.fori_loop(0, EDGE, gradient, 0)
    sums_ref[0:EDGE, :] = fold(rmask * part_ref[:POINTS, :])
    for copy in copies[2:]:
        copy.wait()


def operator_kernel(
    capacity,
    own_rows,
    part_ref,
    grad_first_ref,
    grad_second_ref,
    grad_third_ref,
    diagonal_ref,
    cross_ref,
    known_ref,
    low_ref,
    high_ref,
    corners_ref,
    alive_ref,
    hot_ref,
    coarse_ref,
    direction_ref,
    applied_ref,
    section_out,
    sums_out,
    near_out,
    far_out,
    *refs,
):
    *packed_outs, first_ref, third_ref, slope_ref, rise_ref, pipe_ref = refs
    slots = direction_ref.shape[1]
    backward = DERIVATIVE.T
    alive = alive_ref[...]
    rows = coarse_lookup(coarse_ref[:, :own_rows], low_ref, high_ref, slots)
    rows = [alive * row for row in rows]
    field, along_first, along_second, along_third = lift_corners(rows, slots)
    for i, plane in enumerate(field):
        whole = slice(i * PLANE, (i + 1) * PLANE)
        direction_ref[whole, :] = part_ref[whole, :] + plane
    slope_ref[...] = along_second
    rise_ref[...] = along_third

    def fluxes(step, curvature):
        base = pl.multiple_of(step * PLANE, PLANE)
        whole = pl.ds(base, PLANE)
        line = pl.ds(pl.multiple_of(step * EDGE, EDGE), EDGE)
        field = direction_ref[whole, :]
        slope = slope_ref[line, :]
        rise = rise_ref[line, :]
        grad_first = grad_first_ref[whole, :] + along_first
        grad_second = grad_second_ref[whole, :] + stacked([slope] * EDGE)
        grad_third = grad_third_ref[whole, :] + stacked(
            [jnp.broadcast_to(rise[j : j + 1], (EDGE, slots)) for j in range(EDGE)]
        )
        diagonal = [diagonal_ref[d, whole, :].astype(f32) for d in range(3)]
        cross = [cross_ref[d, whole, :].astype(f32) for d in range(3)]
        flux_first = diagonal[0] * grad_first + cross[0] * grad_second + cross[1] * grad_third
        flux_second = cross[0] * grad_first + diagonal[1] * grad_second + cross[2] * grad_third
        flux_third = cross[1] * grad_first + cross[2] * grad_second + diagonal[2] * grad_third
        energy = (
            grad_first * flux_first
            + grad_second * flux_second
            + grad_third * flux_third
            + field * field
        )
        first_ref[whole, :] = flux_first
        third_ref[whole, :] = flux_third
        rows = [flux_second[j * EDGE : (j + 1) * EDGE] for j in range(EDGE)]
        applied_ref[whole, :] = field + stacked(combine(backward, rows))
        return curvature + fold(energy)

    empty = jnp.zeros((EDGE, slots), f32)
    curvature = lax.fori_loop(0, EDGE, fluxes, empty, unroll=True)
    precond = known_ref[0:EDGE, :] + corners_ref[...] * stacked(rows)
    sums = [precond, curvature, known_ref[EDGE : 2 * EDGE, :]]

    def divergence(step, carry):
        base = pl.multiple_of(step * PLANE, PLANE)
        row = pl.multiple_of(step * EDGE, EDGE)
        for source_ref, places in (
            (first_ref, [pl.ds(i * PLANE + row, EDGE) for i in range(EDGE)]),
            (third_ref, [pl.ds(base + k, EDGE, stride=EDGE) for k in range(EDGE)]),
        ):
            values = combine(backward, [source_ref[place, :] for place in places])
            for place, member in zip(places, values):
                applied_ref[place, :] += member
        return carry

    lax.fori_loop(0, EDGE, divergence, 0, unroll=True)
    pick_faces(applied_ref, hot_ref, capacity, section_out, pipe_ref)
    section = section_out[...]
    for place, packed_out in enumerate(packed_outs):
        packed_out[...] = pack_section(section, place + 1, capacity)
    near_out[...], far_out[...] = pack_pipes(pipe_ref[...])
    row = lane_row([total_of(member) for member in sums])
    sums_out[...] = jnp.broadcast_to(row, sums_out.shape)


def pipe_kernel(applied_ref, codes_ref, hot_ref, near_ref, far_ref, image_ref, grid_ref):
    image_ref[:POINTS, :] = applied_ref[:POINTS, :]
    values = unpacked_pipes(near_ref[...], far_ref[...])
    add_faces(
        image_ref, grid_ref, codes_ref, hot_ref, values, codes_ref.shape[1] - values.shape[1]
    )


def image_kernel(capacity, rmask_ref, partial_ref, codes_ref, hot_ref, sums_ref, *refs):
    *block_refs, image_ref, sums_out, grid_ref = refs
    image_ref[:POINTS, :] = partial_ref[:POINTS, :]
    own_ref, *arrived = block_refs
    values = unpacked_section(
        own_ref[...],
        [block_ref[...] for block_ref in arrived],
        reversed(arrival_order(len(arrived))),
        capacity,
    )
    add_faces(image_ref, grid_ref, codes_ref, hot_ref, values, 0)
    image = image_ref[:POINTS, :]
    rmask = rmask_ref[...]
    square = total_of(image * image)
    product = total_of(rmask * image)
    near = jnp.where(square > 0.0, product / jnp.where(square > 0.0, square, 1.0), 0.0)
    rest = rmask - near * image
    row = lane_row(
        [sums_ref[0:1, n : n + 1] for n in range(3)]
        + [total_of(rest * rest), total_of(rest * image), square, near]
    )
    sums_out[...] = jnp.broadcast_to(row, sums_out.shape)


def update_kernel(
    rmask_ref,
    solution_ref,
    direction_ref,
    image_ref,
    alive_ref,
    sums_ref,
    solution_out,
    residual_out,
    ratio_out,
):
    alive = alive_ref[...]
    sums = sums_ref[...]
    whole = jnp.sum(sums, axis=0, keepdims=True)
    step_length = whole[:, 0:1] / whole[:, 1:2]
    solution_out[...] = alive * (solution_ref[...] + step_length * direction_ref[...])
    residual_out[...] = rmask_ref[...] - step_length * image_ref[:POINTS, :]
    gap = step_length - sums[:, 6:7]
    fresh = sums[:, 3:4] - 2.0 * gap * sums[:, 4:5] + gap * gap * sums[:, 5:6]
    ratio_out[0] = jnp.sum(fresh) / jnp.sum(whole[:, 2:3])


def kernel_call(body, outputs, scratch=(), remote=0, copies=0, leaving=()):
    def call(*operands):
        memory, given = [], []
        for place, operand in enumerate(operands):
            if operand.ndim == 1:
                memory.append(pltpu.SMEM)
            elif place < remote:
                memory.append(pltpu.HBM)
                operand = pltpu.with_memory_space_constraint(operand, pltpu.HBM)
            else:
                memory.append(pltpu.VMEM)
            given.append(operand)
        shapes, spaces = [], []
        for place, output in enumerate(outputs):
            shape, kind = output if isinstance(output[0], tuple) else (output, f32)
            shapes.append(jax.ShapeDtypeStruct(shape, kind))
            if place in leaving:
                spaces.append(pl.ANY)
            else:
                spaces.append(pltpu.SMEM if len(shape) == 1 else pltpu.VMEM)
        return pl.pallas_call(
            body,
            out_shape=tuple(shapes),
            in_specs=[pl.BlockSpec(memory_space=space) for space in memory],
            out_specs=tuple(pl.BlockSpec(memory_space=space) for space in spaces),
            scratch_shapes=[pltpu.VMEM(shape, kind) for shape, kind in scratch]
            + ([pltpu.SemaphoreType.DMA((copies,))] if copies else []),
            compiler_params=pltpu.CompilerParams(vmem_limit_bytes=40 << 20),
        )(*given)

    return call


def held(array):
    return (array.shape, array.dtype)


def exchange(values):
    return lax.all_to_all(values, AXES, split_axis=0, concat_axis=0, tiled=True)


def swap(values, axis, table):
    return lax.ppermute(values, axis, [(int(i), int(table[i])) for i in range(len(table))])


def arrival_order(sections):
    return [0, *range(2, sections), 1]


def swap_faces(section, pipe):
    tables = section_pairings(lax.axis_size("gy"))
    near, far = pairings(lax.axis_size("gx"))
    near_pipe = swap(pipe, "gx", near)
    arrived = [swap(section, "gy", tables[place]) for place in arrival_order(len(tables))]
    return [section, near_pipe, *arrived, swap(pipe, "gx", far)]


def on_device(
    solution,
    residual,
    metric_diag,
    metric_cross,
    fdm_vectors,
    fdm_values,
    vertex_ids,
    coarse_inverse,
    elem_live,
    section_face,
    section_code,
    pipe_face,
    pipe_code,
):
    field = residual.shape
    slots = field[1]
    own_rows, vertices = coarse_inverse.shape
    devices = lax.axis_size(AXES)
    peers, capacity = section_face.shape[1:]
    vectors = fdm_vectors.reshape(-1, slots)
    values = fdm_values.reshape(-1, slots)
    lists = [section_face[0], pipe_face[0]]
    codes = [section_code[0], pipe_code[0]]
    blocks = len(section_pairings(peers)) + 3
    section_width = -(-(blocks - 2) * capacity // LANES) * LANES
    pipe_width = 2 * pipe_face.shape[2]
    width = section_width + pipe_width
    sends = [(PLANE, section_width), (PLANE, pipe_width)]
    grid = ((PLANE * width // LANES + EDGE, LANES), f32)
    tall = (TALL, slots)
    pieces = vertices // LANES
    message = (devices, LANES)

    direct = devices * vertices * 4 <= DIRECT_BYTES
    copies = devices if direct else 1
    given = [elem_live, *lists, vectors, residual, values, vertex_ids]
    terms = (copies, pieces, LANES)
    hot = ((FACES * slots, width), bf16)
    parts, rmask, smooth, section_sent, pipe_sent, alive, hot, vertex_ids, corners = kernel_call(
        smooth_kernel,
        [
            terms,
            field,
            tall,
            *sends,
            (1, slots),
            hot,
            held(vertex_ids),
            (CORNERS, slots),
        ],
        [held(member) for member in [*lists, vectors, values]]
        + [((3 * PLANE, EDGE, slots), f32), (tall, f32), (tall, f32), (terms, f32)],
        remote=len(given),
        copies=len(given),
        leaving=(0,),
    )(*given)
    parts = exchange(parts) if direct else lax.psum(parts, AXES)
    own, near_pipe, *arrived, far_pipe = swap_faces(section_sent, pipe_sent)
    faces = [own, far_pipe, near_pipe, *arrived]
    (coarse,) = kernel_call(coarse_rows_kernel, [message])(coarse_inverse, parts)
    coarse = exchange(coarse)
    corner_count = CORNERS * slots
    known = kernel_call(
        functools.partial(face_kernel, blocks, capacity, own_rows),
        [
            tall,
            tall,
            tall,
            tall,
            held(metric_diag),
            held(metric_cross),
            (2 * EDGE, slots),
            ((own_rows, corner_count), bf16),
            (devices, corner_count),
            ((EDGE, width), jnp.int32),
        ],
        [grid, *(held(member) for member in codes)],
        remote=4,
        copies=4,
    )(metric_diag, metric_cross, *codes, smooth, rmask, vertex_ids, alive, hot, *faces)
    *known, codes = known
    small = (packed_height(capacity), LANES)
    side = (PLANE // 2, LANES)
    direction, applied, own, sums, near_pipe, far_pipe, *packed = kernel_call(
        functools.partial(operator_kernel, capacity, own_rows),
        [field, tall, sends[0], (1, LANES), side, side] + [small] * (blocks - 3),
        [(tall, f32)] * 2 + [((PLANE, slots), f32)] * 2 + [(sends[1], f32)],
    )(*known, corners, alive, hot, coarse)
    tables = section_pairings(peers)
    near, far = pairings(lax.axis_size("gx"))
    order = reversed(arrival_order(len(tables)))
    arrived = [swap(packed[place], "gy", tables[place]) for place in order]
    near_pipe, far_pipe = swap(near_pipe, "gx", near), swap(far_pipe, "gx", far)
    (partial,) = kernel_call(pipe_kernel, [tall], [grid])(
        applied, codes, hot, near_pipe, far_pipe
    )
    image, sums = kernel_call(
        functools.partial(image_kernel, capacity), [tall, message], [grid]
    )(rmask, partial, codes, hot, sums, own, *arrived)
    solution_out, residual_out, norm_ratio = kernel_call(update_kernel, [field, field, (1,)])(
        rmask, solution, direction, image, alive, exchange(sums)
    )
    return (solution_out, residual_out, norm_ratio)


def solution(mesh):
    placed = (
        P(None, AXES),
        P(None, AXES),
        P(None, None, AXES),
        P(None, None, AXES),
        P(None, None, None, AXES),
        P(None, None, AXES),
        P(None, AXES),
        P(AXES, None),
        P(AXES),
        P(AXES, None, None),
        P(AXES, None, None),
        P(AXES, None, None),
        P(AXES, None, None),
    )
    return jax.shard_map(
        on_device,
        mesh=mesh,
        in_specs=placed,
        out_specs=(P(None, AXES), P(None, AXES), P()),
        check_vma=False,
    )
```
